256 devices in a mesh: ex: 16 (over x, z_lo), par: 16 (over y, z_hi, core).
Axes of the slice: x: 4, y: 4, z: 8 (z_hi: 2, z_lo: 4; z = z_hi * 4 + z_lo), core: 2. Of those that a mesh axis runs over, the one named last changes fastest.
Arguments:
- hidden: bfloat16 [16, 512, 8192], P('ex', None, 'par'), may hold values from -6 to 6
- out_grad: bfloat16 [16, 512, 4096], P('ex', None, 'par'), may hold values from -6 to 6
- signed_scale: bfloat16 [8192, 4096], P('par', 'ex'), as said below
- indices: int32 [8192], replicated, may hold values from 0 to 33554431, as said below
Outputs:
- sketch: float32 [16, 8192], P('ex', 'par')
The draws below stay inside these ranges and needn't reach their ends.
Inputs may be any that keep to these rules, and one draw needn't show every extreme that they name: `indices`: strictly increasing; entry k lies in [k * 8192 * 4096 / 8192, (k + 1) * 8192 * 4096 / 8192). `signed_scale`: each entry is plus or minus a factor between 0.2 and 4.
All inputs are finite; a program needn't handle non-finite values.
Results may differ from the reference program's by a relative error of at most 0.0003.
Values may be sent and summed in bfloat16 or wider, within the bound.
A program may use at most 64 MiB of HBM per device.

```python
import math
import jax
import jax.numpy as jnp
from jax import lax

D = 4096
FF = 8192
L = 512
K = 8192
EXAMPLES = 16


def draw_signed_scale(key, part):
    key = jax.random.fold_in(key, 1)
    sign_key, size_key = jax.random.split(key)
    signs_vec = (2 * jax.random.randint(sign_key, (FF, D), 0, 2, dtype=jnp.int32) - 1).astype(jnp.float32)
    magnitude = jnp.exp(jax.random.uniform(size_key, (FF, D), jnp.float32, math.log(0.3), math.log(3.0)))
    return (signs_vec * magnitude).astype(jnp.bfloat16)


def draw_indices(key, part):
    key = jax.random.fold_in(key, 2)
    stride = FF * D // K
    offsets = jax.random.randint(key, (K,), 0, stride, dtype=jnp.int32)
    return jnp.arange(K, dtype=jnp.int32) * stride + offsets


def shard_levels(key, shape, cuts, least, high):
    def one(axis_at, parts):
        steps = jax.random.uniform(jax.random.fold_in(jax.random.fold_in(key, 6), axis_at), (parts,), jnp.float32, least / len(cuts), high / len(cuts))
        return jnp.repeat(jnp.exp(steps), shape[axis_at] // parts).reshape((-1,) + (1,) * (len(shape) - axis_at - 1))

    gain = one(*cuts[0])
    for cut in cuts[1:]:
        gain = gain * one(*cut)
    return gain


def scatter_about(key, extent, spread, bound, shards=(), held_as=jnp.bfloat16):
    level = shard_levels(key, extent, shards, -0.22, 0.18) if shards else 1.0
    array = jax.random.normal(key, extent, jnp.float32) * spread * level
    return jnp.minimum(jnp.maximum(array, -bound), bound).astype(held_as)


def setup_inputs(seed: int = 0) -> dict:
    key_of = jax.random.split(jax.random.key(seed), 5)
    return {
        "hidden": scatter_about(key_of[0], (EXAMPLES, L, FF), 1.0, 6.0, ((0, 16), (2, 16))),
        "out_grad": scatter_about(key_of[1], (EXAMPLES, L, D), 1.0, 6.0, ((0, 16), (2, 16))),
        "signed_scale": draw_signed_scale(jax.random.fold_in(key_of[4], 71), 0),
        "indices": draw_indices(jax.random.fold_in(key_of[4], 71), 0),
    }


def walsh_table(size):
    row_ids = lax.broadcasted_iota(jnp.int32, (size, size), 0)
    col_ids = lax.broadcasted_iota(jnp.int32, (size, size), 1)
    common = jnp.bitwise_and(row_ids, col_ids)
    parity = jnp.zeros((size, size), jnp.int32)
    for bit_pos in range(max(size.bit_length() - 1, 0)):
        parity = parity + jnp.bitwise_and(jnp.right_shift(common, bit_pos), 1)
    return (1 - 2 * jnp.bitwise_and(parity, 1)).astype(jnp.float32)

def factor_list(length):
    factors = []
    remaining = length
    while remaining > 128:
        factors.append(128)
        remaining = remaining // 128
    if remaining > 1:
        factors = [remaining] + factors
    return factors

def walsh_transform(values):
    batch_rows, length = values.shape
    inner_len = length
    for factor_len in factor_list(length):
        inner_len = inner_len // factor_len
        outer_len = length // (factor_len * inner_len)
        signs_table = walsh_table(factor_len)
        if inner_len == 1:
            values = jnp.dot(values.reshape(-1, factor_len), signs_table, precision=lax.Precision.HIGHEST)
        else:
            values = jnp.einsum('bomk,mn->bonk', values.reshape(batch_rows, outer_len, factor_len, inner_len), signs_table, precision=lax.Precision.HIGHEST)
        values = values.reshape(batch_rows, length)
    return values

def reference(hidden, out_grad, signed_scale, indices):
    scale_f32 = signed_scale.astype(jnp.float32)
    out_scale = 1.0 / math.sqrt(FF * D * L)

    def one_example(example_pair):
        activations, cotangent = example_pair
        gradient = jnp.dot(activations.T, cotangent, preferred_element_type=jnp.float32)
        weighted = (gradient * scale_f32).reshape(1, FF * D)
        coeffs = walsh_transform(weighted)
        return jnp.take(coeffs[0], indices) * out_scale
    return lax.map(one_example, (hidden, out_grad))
```

```python
import jax
import jax.numpy as jnp
from jax import lax
from jax.experimental import pallas as pl
from jax.experimental.pallas import tpu as pltpu
from jax.sharding import PartitionSpec as P

MESH = pl.DeviceIdType.MESH
TOKENS = 512
ROWS = 512
COLS = 256
SCALE = 2.0**-17


def parity(bits):
    bits = bits ^ (bits >> 4)
    bits = bits ^ (bits >> 2)
    bits = bits ^ (bits >> 1)
    return bits & 1


def device(x, y, zh, zl, c):
    return (x * 4 + zl, (y * 2 + zh) * 2 + c)


def kernel(hid_hbm, og_hbm, sc_hbm, idx_hbm, out_ref, hid, hid_t, s_buf, o_buf, walsh, idx_rows, idx_wide, idx_cols, acc, red_out, red_in,
           hid_sem, s_sem, o_sem, idx_sem, red_sem, hid_send, s_send, o_send, sx_send, oy_send, oc_send, red_send):
    ex = lax.axis_index("ex")
    par = lax.axis_index("par")
    x, zl = ex // 4, ex % 4
    y, zh, c = par // 4, (par // 2) % 2, par % 2
    zl_lo, zl_hi = zl % 2, zl // 2
    other_zl = zl_hi * 2 + 1 - zl_lo
    s_self = zl_hi == zl_lo
    o_self = zh == zl_lo

    def wait(ref, sem):
        pltpu.make_async_copy(ref, ref, sem).wait()

    own_hid = pltpu.make_async_copy(hid_hbm.at[0], hid.at[zl_lo], hid_sem.at[zl_lo])
    own_hid.start()
    own_idx = pltpu.make_async_copy(idx_hbm, idx_rows, idx_sem)
    own_idx.start()

    barrier = pltpu.get_barrier_semaphore()

    def greet(*place):
        pl.semaphore_signal(barrier, inc=1, device_id=device(*place), device_id_type=MESH)

    greet(x, y, zh, other_zl, c)
    for step in (1, 2, 3):
        greet((x + step) % 4, y, zh, zl, c)
        greet(x, (y + step) % 4, zh, zl, c)
    greet(x, y, zh, zl, 1 - c)
    for d3 in (0, 1):
        source = zl_lo * 2 + d3

        @pl.when(source != zl)
        def _():
            greet(x, y, zh, source, c)

    for e in (0, 1):
        source_zl = zl_hi * 2 + e

        @pl.when(jnp.logical_or(source_zl != zl, zh != zl_lo))
        def _():
            greet(x, y, zl_lo, source_zl, c)

    def greet_group(step, carry):
        there = (par + step) % 16
        pl.semaphore_signal(barrier, inc=1, device_id=(ex, there), device_id_type=MESH)
        return carry

    def greet_other(step, carry):
        there = (par + step) % 16
        pl.semaphore_signal(barrier, inc=1, device_id=(x * 4 + other_zl, there), device_id_type=MESH)
        return carry

    lax.fori_loop(1, 16, greet_group, 0)
    lax.fori_loop(0, 16, greet_other, 0)
    count = 8 + 2 + 2 + 31 - jnp.where(s_self, 1, 0) - jnp.where(o_self, 1, 0)
    pl.semaphore_wait(barrier, count)

    def to_z(src, dst, zh_to, zl_to, send, recv):
        stays = jnp.logical_and(zh_to == zh, zl_to == zl)

        @pl.when(stays)
        def _():
            pltpu.make_async_copy(src, dst, recv).start()

        @pl.when(jnp.logical_not(stays))
        def _():
            pltpu.make_async_remote_copy(src, dst, send, recv, device_id=device(x, y, zh_to, zl_to, c), device_id_type=MESH).start()

    for t in (0, 1):
        to_z(og_hbm.at[0], o_buf.at[zl_lo, y, c], t, zl_hi * 2 + zh, o_send.at[t], o_sem.at[zl_lo, y, c])
        to_z(sc_hbm, s_buf.at[x, zl_lo], zh, t * 2 + zl_hi, s_send.at[t], s_sem.at[x, zl_lo])
    hid_copy = pltpu.make_async_remote_copy(
        hid_hbm.at[0], hid.at[zl_lo], hid_send, hid_sem.at[zl_lo], device_id=device(x, y, zh, other_zl, c), device_id_type=MESH
    )
    hid_copy.start()

    rows = lax.broadcasted_iota(jnp.int32, (COLS, COLS), 0)
    cols = lax.broadcasted_iota(jnp.int32, (COLS, COLS), 1)
    walsh[...] = (1 - 2 * parity(rows & cols)).astype(jnp.float32).astype(jnp.bfloat16)
    acc[...] = jnp.zeros_like(acc)
    own_idx.wait()
    idx_wide[...] = jnp.zeros_like(idx_wide)
    for j in range(16):
        idx_wide[j : j + 1, :] = idx_rows[pl.ds(j * ROWS, ROWS)].reshape(1, ROWS) & 4095
    idx_cols[...] = idx_wide[...].T
    own_hid.wait()
    hid_t[zl_lo] = hid[zl_lo].T

    def s_copy(d3, step):
        return pltpu.make_async_remote_copy(
            s_buf.at[x, d3], s_buf.at[x, d3], sx_send.at[d3, step - 1], s_sem.at[x, d3],
            device_id=device((x + step) % 4, y, zh, zl, c), device_id_type=MESH,
        )

    def o_copy(e, step):
        return pltpu.make_async_remote_copy(
            o_buf.at[e, y, c], o_buf.at[e, y, c], oy_send.at[e, step - 1], o_sem.at[e, y, c],
            device_id=device(x, (y + step) % 4, zh, zl, c), device_id_type=MESH,
        )

    def sibling_copy(e, d1):
        return pltpu.make_async_remote_copy(
            o_buf.at[e, d1, c], o_buf.at[e, d1, c], oc_send.at[e, d1], o_sem.at[e, d1, c],
            device_id=device(x, y, zh, zl, 1 - c), device_id_type=MESH,
        )

    for d3 in (0, 1):
        wait(s_buf.at[x, d3], s_sem.at[x, d3])
        for step in (2, 1, 3):
            s_copy(d3, step).start()
    for e in (0, 1):
        wait(o_buf.at[e, y, c], o_sem.at[e, y, c])
        for step in (2, 1, 3):
            o_copy(e, step).start()
        sibling_copy(e, y).start()

    def tile(e, d1, d3):
        grad = jnp.dot(hid_t[e], o_buf[e, d1, d3], preferred_element_type=jnp.float32)
        weighted = grad * s_buf[d1, d3].astype(jnp.float32)
        top, low = weighted[: ROWS // 2], weighted[ROWS // 2 :]
        for half, part in ((0, top + low), (1, top - low)):
            hi = part.astype(jnp.bfloat16)
            lo = (part - hi.astype(jnp.float32)).astype(jnp.bfloat16)
            mixed = jnp.dot(walsh[...], hi, preferred_element_type=jnp.float32)
            mixed += jnp.dot(walsh[...], lo, preferred_element_type=jnp.float32)
            hi = mixed.astype(jnp.bfloat16)
            lo = (mixed - hi.astype(jnp.float32)).astype(jnp.bfloat16)
            mixed = jnp.dot(hi, walsh[...], preferred_element_type=jnp.float32)
            mixed += jnp.dot(lo, walsh[...], preferred_element_type=jnp.float32)
            span = pl.ds(half * COLS, COLS)
            column = idx_cols[span, :]
            lane = column & 127
            left = jnp.take_along_axis(mixed[:, :128], lane, axis=1)
            right = jnp.take_along_axis(mixed[:, 128:], lane, axis=1)
            block = d1 * 4 + zl_lo * 2 + d3
            odd = parity((column >> 8) & block)
            value = jnp.where((column & 128) == 0, left, right)
            acc[e, span, :] += jnp.where(odd == 0, value, -value)

    def columns(step, carry):
        d1 = (y + step) % 4
        for e in (0, 1):

            @pl.when(step > 0)
            def _():
                wait(o_buf.at[e, d1, c], o_sem.at[e, d1, c])
                sibling_copy(e, d1).start()

        for d3 in (0, 1):

            @pl.when(d1 != x)
            def _():
                wait(s_buf.at[d1, d3], s_sem.at[d1, d3])

        for e in (0, 1):
            wait(o_buf.at[e, d1, 1 - c], o_sem.at[e, d1, 1 - c])

        @pl.when(step == 0)
        def _():
            wait(hid.at[1 - zl_lo], hid_sem.at[1 - zl_lo])
            hid_t[1 - zl_lo] = hid[1 - zl_lo].T

        def pair(at, carry):
            tile(at // 2, d1, at % 2)
            return carry

        lax.fori_loop(0, 4, pair, 0)
        return carry

    lax.fori_loop(0, 4, columns, 0)

    for e in (0, 1):
        lines = acc[e].T
        j = lax.broadcasted_iota(jnp.int32, (16, 128), 0)
        sign = jnp.where(parity(j & par) == 0, SCALE, -SCALE)
        for q in range(4):
            red_out[e, :, q, :] = lines[:16, q * 128 : (q + 1) * 128] * sign

    own_slot = zl_lo * 16 + par
    other_slot = (1 - zl_lo) * 16

    def red_copy(e, ex_to, there, send):
        return pltpu.make_async_remote_copy(
            red_out.at[e, there], red_in.at[own_slot], red_send.at[send], red_sem.at[own_slot],
            device_id=(ex_to, there), device_id_type=MESH,
        )

    def send_group(step, carry):
        there = (par + step) % 16
        red_copy(zl_lo, ex, there, step).start()
        return carry

    def send_other(step, carry):
        there = (par + step) % 16
        red_copy(1 - zl_lo, x * 4 + other_zl, there, 16 + step).start()
        return carry

    lax.fori_loop(0, 16, send_other, 0)
    lax.fori_loop(1, 16, send_group, 0)
    red_in[own_slot] = red_out[zl_lo, par]

    for t in (0, 1):
        zh_to, zl_to = t, zl_hi * 2 + zh

        @pl.when(jnp.logical_or(zh_to != zh, zl_to != zl))
        def _():
            wait(o_buf.at[zl_lo, y, c], o_send.at[t])

        @pl.when(t * 2 + zl_hi != zl)
        def _():
            wait(s_buf.at[x, zl_lo], s_send.at[t])

    hid_copy.wait_send()
    for step in (1, 2, 3):
        for d3 in (0, 1):
            s_copy(d3, step).wait_send()
        for e in (0, 1):
            o_copy(e, step).wait_send()

    def sibling_done(d1, carry):
        for e in (0, 1):
            sibling_copy(e, d1).wait_send()
        return carry

    lax.fori_loop(0, 4, sibling_done, 0)

    def arrived(step, carry):
        there = (par + step) % 16
        wait(red_in.at[other_slot + there], red_sem.at[other_slot + there])

        @pl.when(step > 0)
        def _():
            slot = zl_lo * 16 + there
            wait(red_in.at[slot], red_sem.at[slot])
            red_copy(zl_lo, ex, there, step).wait_send()

        red_copy(1 - zl_lo, x * 4 + other_zl, there, 16 + step).wait_send()
        return carry

    lax.fori_loop(0, 16, arrived, 0)
    total = jnp.sum(red_in[...], axis=0)
    for q in range(4):
        out_ref[:, q * 128 : (q + 1) * 128] = total[q : q + 1, :]


def local(hidden, out_grad, signed_scale, indices):
    dma = pltpu.SemaphoreType.DMA
    bf16, f32, i32 = jnp.bfloat16, jnp.float32, jnp.int32
    return pl.pallas_call(
        kernel,
        out_shape=jax.ShapeDtypeStruct((1, ROWS), f32),
        in_specs=[pl.BlockSpec(memory_space=pl.ANY)] * 4,
        out_specs=pl.BlockSpec(memory_space=pltpu.VMEM),
        scratch_shapes=[
            pltpu.VMEM((2, TOKENS, ROWS), bf16),
            pltpu.VMEM((2, ROWS, TOKENS), bf16),
            pltpu.VMEM((4, 2, ROWS, COLS), bf16),
            pltpu.VMEM((2, 4, 2, TOKENS, COLS), bf16),
            pltpu.VMEM((COLS, COLS), bf16),
            pltpu.VMEM((8192,), i32),
            pltpu.VMEM((128, ROWS), i32),
            pltpu.VMEM((ROWS, 128), i32),
            pltpu.VMEM((2, ROWS, 128), f32),
            pltpu.VMEM((2, 16, 4, 128), f32),
            pltpu.VMEM((32, 4, 128), f32),
            dma((2,)),
            dma((4, 2)),
            dma((2, 4, 2)),
            dma(()),
            dma((32,)),
            dma(()),
            dma((2,)),
            dma((2,)),
            dma((2, 3)),
            dma((2, 3)),
            dma((2, 4)),
            dma((32,)),
        ],
        compiler_params=pltpu.CompilerParams(collective_id=0, has_side_effects=True, vmem_limit_bytes=48 << 20),
        cost_estimate=pl.CostEstimate(flops=6 << 30, bytes_accessed=8 << 20, transcendentals=0),
    )(hidden, out_grad, signed_scale, indices)


def solution(mesh):
    in_specs = (P("ex", None, "par"), P("ex", None, "par"), P("par", "ex"), P())
    out_specs = P("ex", "par")
    return jax.shard_map(local, mesh=mesh, in_specs=in_specs, out_specs=out_specs, check_vma=False)
```

```python
import jax
import jax.numpy as jnp
from jax import lax
from jax.experimental import pallas as pl
from jax.experimental.pallas import tpu as pltpu
from jax.sharding import PartitionSpec as P

MESH = pl.DeviceIdType.MESH
TOKENS = 512
ROWS = 512
COLS = 256
SCALE = 2.0**-17
CHUNKS = 4
WINDOW = 4
HIDDEN_AT = 3
SLAB = 512 // CHUNKS


def parity(bits):
    bits = bits ^ (bits >> 4)
    bits = bits ^ (bits >> 2)
    bits = bits ^ (bits >> 1)
    return bits & 1


def wrap(value, size):
    return jnp.where(value >= size, value - size, value)


def kernel(hid_hbm, og_hbm, sc_hbm, idx_hbm, out_ref, hid, hid_t, s_buf, o_buf, walsh, walsh_tall, idx_rows, idx_wide, idx_cols, acc,
           red_out, red_in, hid_sem, sz_sem, sx_sem, sf_sem, oz_sem, oy_sem, of_sem, sib_sem, idx_sem, red_sem, hid_send, s_send,
           o_send, sx_send, sf_send, oy_send, of_send, sib_send, red_send):
    ex = lax.axis_index("ex")
    par = lax.axis_index("par")
    x = ex // 4
    zl = ex - x * 4
    y = par // 4
    rest = par - y * 4
    zh = rest // 2
    c = rest - zh * 2
    zl_hi = zl // 2
    zl_lo = zl - zl_hi * 2
    other_lo = 1 - zl_lo
    other_ex = ex + 1 - 2 * zl_lo
    xs = [x, wrap(x + 1, 4), wrap(x + 2, 4), wrap(x + 3, 4)]
    ys = [y, wrap(y + 1, 4), wrap(y + 2, 4), wrap(y + 3, 4)]
    x_dev = [(ex + (v - x) * 4, par) for v in xs]
    y_dev = [(ex, par + (v - y) * 4) for v in ys]
    sib_dev = (ex, par + 1 - 2 * c)
    hid_dev = (other_ex, par)
    s_to = [2 * t + zl_hi for t in (0, 1)]
    s_from = [2 * zl_lo + d3 for d3 in (0, 1)]
    o_to_zl = zl_hi * 2 + zh
    o_from_zl = [zl_hi * 2 + e for e in (0, 1)]
    o_self = zh == zl_lo
    s_self = zl_hi == zl_lo

    def wait(ref, sem):
        pltpu.make_async_copy(ref, ref, sem).wait()

    def remote(src, dst, send, recv, place):
        return pltpu.make_async_remote_copy(src, dst, send, recv, device_id=place, device_id_type=MESH)

    barrier = pltpu.get_barrier_semaphore()

    def greet(place):
        pl.semaphore_signal(barrier, inc=1, device_id=place, device_id_type=MESH)

    for place in x_dev[1:] + y_dev[1:] + [sib_dev, hid_dev]:
        greet(place)
    for d3 in (0, 1):

        @pl.when(s_from[d3] != zl)
        def _():
            greet((x * 4 + s_from[d3], par))

    for e in (0, 1):

        @pl.when(jnp.logical_not(jnp.logical_and(o_self, zl_lo == e)))
        def _():
            greet((x * 4 + o_from_zl[e], y * 4 + zl_lo * 2 + c))

    for step in range(16):
        there = wrap(par + step, 16)
        if step > 0:
            greet((ex, there))
        greet((other_ex, there))

    own_hid = pltpu.make_async_copy(hid_hbm.at[0], hid.at[zl_lo], hid_sem.at[zl_lo])
    own_hid.start()
    own_idx = pltpu.make_async_copy(idx_hbm, idx_rows, idx_sem)
    own_idx.start()
    rows = lax.broadcasted_iota(jnp.int32, (COLS, COLS), 0)
    cols = lax.broadcasted_iota(jnp.int32, (COLS, COLS), 1)
    signs = (1 - 2 * parity(rows & cols)).astype(jnp.float32).astype(jnp.bfloat16)
    for half in (0, 1):
        walsh[:, half * COLS : (half + 1) * COLS] = signs
        walsh_tall[half * COLS : (half + 1) * COLS, :] = signs
    acc[...] = jnp.zeros_like(acc)
    own_idx.wait()
    idx_wide[...] = jnp.zeros_like(idx_wide)
    for j in range(16):
        idx_wide[j : j + 1, :] = idx_rows[pl.ds(j * ROWS, ROWS)].reshape(1, ROWS) & 4095
    idx_cols[...] = idx_wide[...].T
    own_hid.wait()
    hid_t[zl_lo] = hid[zl_lo].T
    pl.semaphore_wait(barrier, 43 - jnp.where(s_self, 1, 0) - jnp.where(o_self, 1, 0))

    def slab(i):
        return pl.ds(i * SLAB, SLAB)

    def along_z(i, start):
        for t in (0, 1):
            args = (og_hbm.at[0, slab(i)], o_buf.at[zl_lo, y, c, slab(i)])
            send, recv = o_send.at[t, i], oz_sem.at[zl_lo, i]
            stays = jnp.logical_and(o_self, zh == t)

            @pl.when(jnp.logical_not(stays))
            def _():
                copy = remote(*args, send, recv, (x * 4 + o_to_zl, y * 4 + t * 2 + c))
                if start:
                    copy.start()
                else:
                    copy.wait_send()

            if start:

                @pl.when(stays)
                def _():
                    pltpu.make_async_copy(*args, recv).start()

        for t in (0, 1):
            s_args = (sc_hbm.at[slab(i)], s_buf.at[x, zl_lo, slab(i)])
            s_s, s_r = s_send.at[t, i], sz_sem.at[zl_lo, i]

            @pl.when(s_to[t] != zl)
            def _():
                copy = remote(*s_args, s_s, s_r, (x * 4 + s_to[t], par))
                if start:
                    copy.start()
                else:
                    copy.wait_send()

            if start:

                @pl.when(s_to[t] == zl)
                def _():
                    pltpu.make_async_copy(*s_args, s_r).start()

    hid_copy = remote(hid_hbm.at[0], hid.at[zl_lo], hid_send, hid_sem.at[zl_lo], hid_dev)

    def sx_copy(step, i):
        ref = s_buf.at[x, :, slab(i)]
        return remote(ref, ref, sx_send, sx_sem.at[step // 2, i], x_dev[step])

    def sf_copy(step, i):
        ref = s_buf.at[xs[4 - step], step // 2, slab(i)]
        return remote(ref, ref, sf_send, sf_sem.at[step // 2, i], x_dev[step])

    def oy_copy(step, i):
        ref = o_buf.at[:, y, c, slab(i)]
        return remote(ref, ref, oy_send, oy_sem.at[step // 2, i], y_dev[step])

    def of_copy(step, i):
        ref = o_buf.at[step // 2, ys[4 - step], c, slab(i)]
        return remote(ref, ref, of_send, of_sem.at[step // 2, i], y_dev[step])

    def sib_copy(step, i):
        ref = o_buf.at[:, ys[step], c, slab(i)]
        return remote(ref, ref, sib_send, sib_sem.at[step, i], sib_dev)

    def first(i):
        for d3 in (0, 1):
            wait(s_buf.at[x, d3, slab(i)], sz_sem.at[d3, i])
        for step in (1, 3):
            sx_copy(step, i).start()
        for e in (0, 1):
            wait(o_buf.at[e, y, c, slab(i)], oz_sem.at[e, i])
        for step in (1, 3):
            oy_copy(step, i).start()
        sib_copy(0, i).start()

    def second(i):
        for step in (1, 3):
            wait(s_buf.at[xs[4 - step], :, slab(i)], sx_sem.at[step // 2, i])
            sf_copy(step, i).start()
            wait(o_buf.at[:, ys[4 - step], c, slab(i)], oy_sem.at[step // 2, i])
            of_copy(step, i).start()
            sib_copy(4 - step, i).start()

    def third(i):
        for e in (0, 1):
            wait(o_buf.at[e, ys[2], c, slab(i)], of_sem.at[e, i])
        sib_copy(2, i).start()

    for i in range(min(WINDOW, CHUNKS)):
        along_z(i, True)
    for i in range(CHUNKS + 2):
        if i < CHUNKS:
            first(i)
        if i == HIDDEN_AT:
            hid_copy.start()
        if i < CHUNKS - WINDOW:
            along_z(i, False)
            along_z(i + WINDOW, True)
        if 0 < i <= CHUNKS:
            second(i - 1)
        if i > 1:
            third(i - 2)
    for i in range(CHUNKS):
        for d3 in (0, 1):
            wait(s_buf.at[xs[2], d3, slab(i)], sf_sem.at[d3, i])

    def tile(e, d1, d3):
        grad = jnp.dot(hid_t[e], o_buf[e, d1, d3], preferred_element_type=jnp.float32)
        weighted = grad * s_buf[d1, d3].astype(jnp.float32)
        top, low = weighted[: ROWS // 2], weighted[ROWS // 2 :]
        for half, part in ((0, top + low), (1, top - low)):
            hi = part.astype(jnp.bfloat16)
            lo = (part - hi.astype(jnp.float32)).astype(jnp.bfloat16)
            mixed = jnp.dot(walsh[...], jnp.concatenate([hi, lo], axis=0), preferred_element_type=jnp.float32)
            hi = mixed.astype(jnp.bfloat16)
            lo = (mixed - hi.astype(jnp.float32)).astype(jnp.bfloat16)
            mixed = jnp.dot(jnp.concatenate([hi, lo], axis=1), walsh_tall[...], preferred_element_type=jnp.float32)
            span = pl.ds(half * COLS, COLS)
            column = idx_cols[span, :]
            lane = column & 127
            left = jnp.take_along_axis(mixed[:, :128], lane, axis=1)
            right = jnp.take_along_axis(mixed[:, 128:], lane, axis=1)
            block = d1 * 4 + zl_lo * 2 + d3
            odd = parity((column >> 8) & block)
            value = jnp.where((column & 128) == 0, left, right)
            acc[e, span, :] += jnp.where(odd == 0, value, -value)

    def column_pair(e, step):
        d1 = wrap(y + step, 4)
        for d3 in (0, 1):
            tile(e, d1, d3)

    def own_columns(step, carry):
        for i in range(CHUNKS):
            wait(o_buf.at[:, wrap(y + step, 4), 1 - c, slab(i)], sib_sem.at[step, i])
        column_pair(zl_lo, step)
        return carry

    lax.fori_loop(0, 4, own_columns, 0)

    own_slot = zl_lo * 16 + par
    other_slot = other_lo * 16

    def gather_picks(e):
        lines = acc[e].T
        j = lax.broadcasted_iota(jnp.int32, (16, 128), 0)
        sign = jnp.where(parity(j & par) == 0, SCALE, -SCALE)
        for q in range(4):
            red_out[e, :, q, :] = lines[:16, q * 128 : (q + 1) * 128] * sign

    def red_copy(e, step):
        there = wrap(par + step, 16)
        place = (jnp.where(e == zl_lo, ex, other_ex), there)
        return remote(red_out.at[e, there], red_in.at[own_slot], red_send, red_sem.at[own_slot], place)

    gather_picks(zl_lo)
    for step in range(1, 16):
        red_copy(zl_lo, step).start()
    red_in[own_slot] = red_out[zl_lo, par]

    wait(hid.at[other_lo], hid_sem.at[other_lo])
    hid_t[other_lo] = hid[other_lo].T

    def other_columns(step, carry):
        column_pair(other_lo, step)
        return carry

    lax.fori_loop(0, 4, other_columns, 0)
    gather_picks(other_lo)
    for step in range(16):
        red_copy(other_lo, step).start()

    for i in range(max(CHUNKS - WINDOW, 0), CHUNKS):
        along_z(i, False)
    hid_copy.wait_send()
    wait(s_buf.at[0:2], sx_send)
    wait(s_buf.at[0], sf_send)
    wait(s_buf.at[0:2], oy_send)
    wait(s_buf.at[0], of_send)
    wait(s_buf, sib_send)

    for step in range(16):
        there = wrap(par + step, 16)
        wait(red_in.at[other_slot + there], red_sem.at[other_slot + there])
        if step > 0:
            slot = zl_lo * 16 + there
            wait(red_in.at[slot], red_sem.at[slot])
    wait(red_in.at[0:31], red_send)
    total = jnp.sum(red_in[...], axis=0)
    for q in range(4):
        out_ref[:, q * 128 : (q + 1) * 128] = total[q : q + 1, :]


def local(hidden, out_grad, signed_scale, indices):
    dma = pltpu.SemaphoreType.DMA
    bf16, f32, i32 = jnp.bfloat16, jnp.float32, jnp.int32
    return pl.pallas_call(
        kernel,
        out_shape=jax.ShapeDtypeStruct((1, ROWS), f32),
        in_specs=[pl.BlockSpec(memory_space=pltpu.HBM)] * 4,
        out_specs=pl.BlockSpec(memory_space=pltpu.VMEM),
        scratch_shapes=[
            pltpu.VMEM((2, TOKENS, ROWS), bf16),
            pltpu.VMEM((2, ROWS, TOKENS), bf16),
            pltpu.VMEM((4, 2, ROWS, COLS), bf16),
            pltpu.VMEM((2, 4, 2, TOKENS, COLS), bf16),
            pltpu.VMEM((COLS, 2 * COLS), bf16),
            pltpu.VMEM((2 * COLS, COLS), bf16),
            pltpu.VMEM((8192,), i32),
            pltpu.VMEM((128, ROWS), i32),
            pltpu.VMEM((ROWS, 128), i32),
            pltpu.VMEM((2, ROWS, 128), f32),
            pltpu.VMEM((2, 16, 4, 128), f32),
            pltpu.VMEM((32, 4, 128), f32),
            dma((2,)),
            dma((2, CHUNKS)),
            dma((2, CHUNKS)),
            dma((2, CHUNKS)),
            dma((2, CHUNKS)),
            dma((2, CHUNKS)),
            dma((2, CHUNKS)),
            dma((4, CHUNKS)),
            dma(()),
            dma((32,)),
            dma(()),
            dma((2, CHUNKS)),
            dma((2, CHUNKS)),
            dma(()),
            dma(()),
            dma(()),
            dma(()),
            dma(()),
            dma(()),
        ],
        compiler_params=pltpu.CompilerParams(collective_id=0, has_side_effects=True, vmem_limit_bytes=56 << 20),
        cost_estimate=pl.CostEstimate(flops=6 << 30, bytes_accessed=8 << 20, transcendentals=0),
    )(hidden, out_grad, signed_scale, indices)


def solution(mesh):
    in_specs = (P("ex", None, "par"), P("ex", None, "par"), P("par", "ex"), P())
    out_specs = P("ex", "par")
    return jax.shard_map(local, mesh=mesh, in_specs=in_specs, out_specs=out_specs, check_vma=False)
```

```python
import jax
import jax.numpy as jnp
from jax import lax
from jax.experimental import pallas as pl
from jax.experimental.pallas import tpu as pltpu
from jax.sharding import PartitionSpec as P

MESH = pl.DeviceIdType.MESH
TOKENS = 512
ROWS = 512
COLS = 256
SCALE = 2.0**-17
CHUNKS = 4
WINDOW = 4
HIDDEN_AT = 3
SLAB = 512 // CHUNKS


def parity(bits):
    bits = bits ^ (bits >> 4)
    bits = bits ^ (bits >> 2)
    bits = bits ^ (bits >> 1)
    return bits & 1


def wrap(value, size):
    return jnp.where(value >= size, value - size, value)


def kernel(hid_hbm, og_hbm, sc_hbm, idx_hbm, out_ref, hid, hid_t, s_buf, o_buf, walsh, walsh_tall, idx_rows, idx_wide, idx_cols, acc,
           red_out, red_in, hid_sem, sz_sem, sx_sem, sf_sem, oz_sem, oy_sem, of_sem, sib_sem, idx_sem, red_sem, hid_send, s_send,
           o_send, sx_send, sf_send, oy_send, of_send, sib_send, red_send):
    ex = lax.axis_index("ex")
    par = lax.axis_index("par")
    x = ex // 4
    zl = ex - x * 4
    y = par // 4
    rest = par - y * 4
    zh = rest // 2
    c = rest - zh * 2
    zl_hi = zl // 2
    zl_lo = zl - zl_hi * 2
    other_lo = 1 - zl_lo
    other_ex = ex + 1 - 2 * zl_lo
    xs = [x, wrap(x + 1, 4), wrap(x + 2, 4), wrap(x + 3, 4)]
    ys = [y, wrap(y + 1, 4), wrap(y + 2, 4), wrap(y + 3, 4)]
    x_dev = [(ex + (v - x) * 4, par) for v in xs]
    y_dev = [(ex, par + (v - y) * 4) for v in ys]
    sib_dev = (ex, par + 1 - 2 * c)
    hid_dev = (other_ex, par)
    s_to = [2 * t + zl_hi for t in (0, 1)]
    s_from = [2 * zl_lo + d3 for d3 in (0, 1)]
    o_to_zl = zl_hi * 2 + zh
    o_from_zl = [zl_hi * 2 + e for e in (0, 1)]
    o_self = zh == zl_lo
    s_self = zl_hi == zl_lo

    def wait(ref, sem):
        pltpu.make_async_copy(ref, ref, sem).wait()

    def remote(src, dst, send, recv, place):
        return pltpu.make_async_remote_copy(src, dst, send, recv, device_id=place, device_id_type=MESH)

    barrier = pltpu.get_barrier_semaphore()

    def greet(place):
        pl.semaphore_signal(barrier, inc=1, device_id=place, device_id_type=MESH)

    for place in x_dev[1:] + y_dev[1:] + [sib_dev, hid_dev]:
        greet(place)
    for d3 in (0, 1):

        @pl.when(s_from[d3] != zl)
        def _():
            greet((x * 4 + s_from[d3], par))

    for e in (0, 1):

        @pl.when(jnp.logical_not(jnp.logical_and(o_self, zl_lo == e)))
        def _():
            greet((x * 4 + o_from_zl[e], y * 4 + zl_lo * 2 + c))

    own_hid = pltpu.make_async_copy(hid_hbm.at[0], hid.at[zl_lo], hid_sem.at[zl_lo])
    own_hid.start()
    own_idx = pltpu.make_async_copy(idx_hbm, idx_rows, idx_sem)
    own_idx.start()
    rows = lax.broadcasted_iota(jnp.int32, (COLS, COLS), 0)
    cols = lax.broadcasted_iota(jnp.int32, (COLS, COLS), 1)
    signs = (1 - 2 * parity(rows & cols)).astype(jnp.float32).astype(jnp.bfloat16)
    for half in (0, 1):
        walsh[:, half * COLS : (half + 1) * COLS] = signs
        walsh_tall[half * COLS : (half + 1) * COLS, :] = signs
    acc[...] = jnp.zeros_like(acc)
    own_idx.wait()
    idx_wide[...] = jnp.zeros_like(idx_wide)
    for j in range(16):
        idx_wide[j : j + 1, :] = idx_rows[pl.ds(j * ROWS, ROWS)].reshape(1, ROWS) & 4095
    idx_cols[...] = idx_wide[...].T
    own_hid.wait()
    hid_t[zl_lo] = hid[zl_lo].T
    pl.semaphore_wait(barrier, 12 - jnp.where(s_self, 1, 0) - jnp.where(o_self, 1, 0))

    def slab(i):
        return pl.ds(i * SLAB, SLAB)

    def along_z(i, start):
        for t in (0, 1):
            args = (og_hbm.at[0, slab(i)], o_buf.at[zl_lo, y, c, slab(i)])
            send, recv = o_send.at[t, i], oz_sem.at[zl_lo, i]
            stays = jnp.logical_and(o_self, zh == t)

            @pl.when(jnp.logical_not(stays))
            def _():
                copy = remote(*args, send, recv, (x * 4 + o_to_zl, y * 4 + t * 2 + c))
                if start:
                    copy.start()
                else:
                    copy.wait_send()

            if start:

                @pl.when(stays)
                def _():
                    pltpu.make_async_copy(*args, recv).start()

        for t in (0, 1):
            s_args = (sc_hbm.at[slab(i)], s_buf.at[x, zl_lo, slab(i)])
            s_s, s_r = s_send.at[t, i], sz_sem.at[zl_lo, i]

            @pl.when(s_to[t] != zl)
            def _():
                copy = remote(*s_args, s_s, s_r, (x * 4 + s_to[t], par))
                if start:
                    copy.start()
                else:
                    copy.wait_send()

            if start:

                @pl.when(s_to[t] == zl)
                def _():
                    pltpu.make_async_copy(*s_args, s_r).start()

    hid_copy = remote(hid_hbm.at[0], hid.at[zl_lo], hid_send, hid_sem.at[zl_lo], hid_dev)

    def sx_copy(step, i):
        ref = s_buf.at[x, :, slab(i)]
        return remote(ref, ref, sx_send, sx_sem.at[step // 2, i], x_dev[step])

    def sf_copy(step, i):
        ref = s_buf.at[xs[4 - step], step // 2, slab(i)]
        return remote(ref, ref, sf_send, sf_sem.at[step // 2, i], x_dev[step])

    def oy_copy(step, i):
        ref = o_buf.at[:, y, c, slab(i)]
        return remote(ref, ref, oy_send, oy_sem.at[step // 2, i], y_dev[step])

    def of_copy(step, i):
        ref = o_buf.at[step // 2, ys[4 - step], c, slab(i)]
        return remote(ref, ref, of_send, of_sem.at[step // 2, i], y_dev[step])

    def sib_copy(step, i):
        ref = o_buf.at[:, ys[step], c, slab(i)]
        return remote(ref, ref, sib_send, sib_sem.at[step, i], sib_dev)

    def sib_wait(step, i):
        wait(o_buf.at[:, wrap(y + step, 4), 1 - c, slab(i)], sib_sem.at[step, i])

    def first(i):
        for d3 in (0, 1):
            wait(s_buf.at[x, d3, slab(i)], sz_sem.at[d3, i])
        for step in (1, 3):
            sx_copy(step, i).start()
        for e in (0, 1):
            wait(o_buf.at[e, y, c, slab(i)], oz_sem.at[e, i])
        for step in (1, 3):
            oy_copy(step, i).start()
        sib_copy(0, i).start()

    def second(i):
        for step in (1, 3):
            wait(s_buf.at[xs[4 - step], :, slab(i)], sx_sem.at[step // 2, i])
            sf_copy(step, i).start()
            wait(o_buf.at[:, ys[4 - step], c, slab(i)], oy_sem.at[step // 2, i])
            of_copy(step, i).start()
            sib_copy(4 - step, i).start()

    def third(i):
        for e in (0, 1):
            wait(o_buf.at[e, ys[2], c, slab(i)], of_sem.at[e, i])
        sib_copy(2, i).start()

    for i in range(min(WINDOW, CHUNKS)):
        along_z(i, True)
    for i in range(CHUNKS + 2):
        if i < CHUNKS:
            first(i)
        if i == HIDDEN_AT:
            for step in range(4):
                sib_wait(step, 0)
            hid_copy.start()
        if i < CHUNKS - WINDOW:
            along_z(i, False)
            along_z(i + WINDOW, True)
        if 0 < i <= CHUNKS:
            second(i - 1)
        if i > 1:
            third(i - 2)
    for i in range(CHUNKS):
        for d3 in (0, 1):
            wait(s_buf.at[xs[2], d3, slab(i)], sf_sem.at[d3, i])

    def tile(e, d1, d3):
        grad = jnp.dot(hid_t[e], o_buf[e, d1, d3], preferred_element_type=jnp.float32)
        weighted = grad * s_buf[d1, d3].astype(jnp.float32)
        top, low = weighted[: ROWS // 2], weighted[ROWS // 2 :]
        for half, part in ((0, top + low), (1, top - low)):
            hi = part.astype(jnp.bfloat16)
            lo = (part - hi.astype(jnp.float32)).astype(jnp.bfloat16)
            mixed = jnp.dot(walsh[...], jnp.concatenate([hi, lo], axis=0), preferred_element_type=jnp.float32)
            hi = mixed.astype(jnp.bfloat16)
            lo = (mixed - hi.astype(jnp.float32)).astype(jnp.bfloat16)
            mixed = jnp.dot(jnp.concatenate([hi, lo], axis=1), walsh_tall[...], preferred_element_type=jnp.float32)
            span = pl.ds(half * COLS, COLS)
            column = idx_cols[span, :]
            lane = column & 127
            left = jnp.take_along_axis(mixed[:, :128], lane, axis=1)
            right = jnp.take_along_axis(mixed[:, 128:], lane, axis=1)
            block = d1 * 4 + zl_lo * 2 + d3
            odd = parity((column >> 8) & block)
            value = jnp.where((column & 128) == 0, left, right)
            acc[e, span, :] += jnp.where(odd == 0, value, -value)

    def column_pair(e, step):
        d1 = wrap(y + step, 4)
        for d3 in (0, 1):
            tile(e, d1, d3)

    def own_columns(step, carry):
        for i in range(1, CHUNKS):
            sib_wait(step, i)
        column_pair(zl_lo, step)
        return carry

    lax.fori_loop(0, 4, own_columns, 0)

    own_slot = zl_lo * 16 + par
    other_slot = other_lo * 16

    def gather_picks(e):
        lines = acc[e].T
        j = lax.broadcasted_iota(jnp.int32, (16, 128), 0)
        sign = jnp.where(parity(j & par) == 0, SCALE, -SCALE)
        for q in range(4):
            red_out[e, :, q, :] = lines[:16, q * 128 : (q + 1) * 128] * sign

    def red_copy(e, step):
        there = wrap(par + step, 16)
        place = (jnp.where(e == zl_lo, ex, other_ex), there)
        return remote(red_out.at[e, there], red_in.at[own_slot], red_send, red_sem.at[own_slot], place)

    gather_picks(zl_lo)
    for step in range(1, 16):
        red_copy(zl_lo, step).start()
    red_in[own_slot] = red_out[zl_lo, par]

    wait(hid.at[other_lo], hid_sem.at[other_lo])
    hid_t[other_lo] = hid[other_lo].T

    def other_columns(step, carry):
        column_pair(other_lo, step)
        return carry

    lax.fori_loop(0, 4, other_columns, 0)
    gather_picks(other_lo)
    for step in range(16):
        red_copy(other_lo, step).start()

    for i in range(max(CHUNKS - WINDOW, 0), CHUNKS):
        along_z(i, False)
    hid_copy.wait_send()
    wait(s_buf.at[0:2], sx_send)
    wait(s_buf.at[0], sf_send)
    wait(s_buf.at[0:2], oy_send)
    wait(s_buf.at[0], of_send)
    wait(s_buf, sib_send)

    for step in range(16):
        there = wrap(par + step, 16)
        wait(red_in.at[other_slot + there], red_sem.at[other_slot + there])
        if step > 0:
            slot = zl_lo * 16 + there
            wait(red_in.at[slot], red_sem.at[slot])
    wait(red_in.at[0:31], red_send)
    total = jnp.sum(red_in[...], axis=0)
    for q in range(4):
        out_ref[:, q * 128 : (q + 1) * 128] = total[q : q + 1, :]


def local(hidden, out_grad, signed_scale, indices):
    dma = pltpu.SemaphoreType.DMA
    bf16, f32, i32 = jnp.bfloat16, jnp.float32, jnp.int32
    return pl.pallas_call(
        kernel,
        out_shape=jax.ShapeDtypeStruct((1, ROWS), f32),
        in_specs=[pl.BlockSpec(memory_space=pltpu.HBM)] * 4,
        out_specs=pl.BlockSpec(memory_space=pltpu.VMEM),
        scratch_shapes=[
            pltpu.VMEM((2, TOKENS, ROWS), bf16),
            pltpu.VMEM((2, ROWS, TOKENS), bf16),
            pltpu.VMEM((4, 2, ROWS, COLS), bf16),
            pltpu.VMEM((2, 4, 2, TOKENS, COLS), bf16),
            pltpu.VMEM((COLS, 2 * COLS), bf16),
            pltpu.VMEM((2 * COLS, COLS), bf16),
            pltpu.VMEM((8192,), i32),
            pltpu.VMEM((128, ROWS), i32),
            pltpu.VMEM((ROWS, 128), i32),
            pltpu.VMEM((2, ROWS, 128), f32),
            pltpu.VMEM((2, 16, 4, 128), f32),
            pltpu.VMEM((32, 4, 128), f32),
            dma((2,)),
            dma((2, CHUNKS)),
            dma((2, CHUNKS)),
            dma((2, CHUNKS)),
            dma((2, CHUNKS)),
            dma((2, CHUNKS)),
            dma((2, CHUNKS)),
            dma((4, CHUNKS)),
            dma(()),
            dma((32,)),
            dma(()),
            dma((2, CHUNKS)),
            dma((2, CHUNKS)),
            dma(()),
            dma(()),
            dma(()),
            dma(()),
            dma(()),
            dma(()),
        ],
        compiler_params=pltpu.CompilerParams(collective_id=0, has_side_effects=True, vmem_limit_bytes=56 << 20),
        cost_estimate=pl.CostEstimate(flops=6 << 30, bytes_accessed=8 << 20, transcendentals=0),
    )(hidden, out_grad, signed_scale, indices)


def solution(mesh):
    in_specs = (P("ex", None, "par"), P("ex", None, "par"), P("par", "ex"), P())
    out_specs = P("ex", "par")
    return jax.shard_map(local, mesh=mesh, in_specs=in_specs, out_specs=out_specs, check_vma=False)
```

```python
import jax
import jax.numpy as jnp
from jax import lax
from jax.experimental import pallas as pl
from jax.experimental.pallas import tpu as pltpu
from jax.sharding import PartitionSpec as P

MESH = pl.DeviceIdType.MESH
TOKENS = 512
ROWS = 512
COLS = 256
SCALE = 2.0**-17
CHUNKS = 4
WINDOW = 4
HIDDEN_AT = 3
SLAB = 512 // CHUNKS


def parity(bits):
    bits = bits ^ (bits >> 4)
    bits = bits ^ (bits >> 2)
    bits = bits ^ (bits >> 1)
    return bits & 1


def wrap(value, size):
    return jnp.where(value >= size, value - size, value)


def kernel(hid_hbm, og_hbm, sc_hbm, idx_hbm, out_ref, hid, hid_t, s_buf, o_buf, walsh, walsh_tall, idx_rows, idx_wide, idx_cols, acc,
           red_out, red_in, hid_sem, sz_sem, sx_sem, sf_sem, oz_sem, oy_sem, of_sem, sib_sem, idx_sem, red_sem, hid_send, s_send,
           o_send, sx_send, sf_send, oy_send, of_send, sib_send, red_send):
    ex = lax.axis_index("ex")
    par = lax.axis_index("par")
    x = ex // 4
    zl = ex - x * 4
    y = par // 4
    rest = par - y * 4
    zh = rest // 2
    c = rest - zh * 2
    zl_hi = zl // 2
    zl_lo = zl - zl_hi * 2
    other_lo = 1 - zl_lo
    other_ex = ex + 1 - 2 * zl_lo
    xs = [x, wrap(x + 1, 4), wrap(x + 2, 4), wrap(x + 3, 4)]
    ys = [y, wrap(y + 1, 4), wrap(y + 2, 4), wrap(y + 3, 4)]
    x_dev = [(ex + (v - x) * 4, par) for v in xs]
    y_dev = [(ex, par + (v - y) * 4) for v in ys]
    sib_dev = (ex, par + 1 - 2 * c)
    hid_dev = (other_ex, par)
    s_to = [2 * t + zl_hi for t in (0, 1)]
    s_from = [2 * zl_lo + d3 for d3 in (0, 1)]
    o_to_zl = zl_hi * 2 + zh
    o_from_zl = [zl_hi * 2 + e for e in (0, 1)]
    o_self = zh == zl_lo
    s_self = zl_hi == zl_lo

    def wait(ref, sem):
        pltpu.make_async_copy(ref, ref, sem).wait()

    def remote(src, dst, send, recv, place):
        return pltpu.make_async_remote_copy(src, dst, send, recv, device_id=place, device_id_type=MESH)

    barrier = pltpu.get_barrier_semaphore()

    def greet(place):
        pl.semaphore_signal(barrier, inc=1, device_id=place, device_id_type=MESH)

    for place in x_dev[1:] + y_dev[1:] + [sib_dev, hid_dev]:
        greet(place)
    for d3 in (0, 1):

        @pl.when(s_from[d3] != zl)
        def _():
            greet((x * 4 + s_from[d3], par))

    for e in (0, 1):

        @pl.when(jnp.logical_not(jnp.logical_and(o_self, zl_lo == e)))
        def _():
            greet((x * 4 + o_from_zl[e], y * 4 + zl_lo * 2 + c))

    own_hid = pltpu.make_async_copy(hid_hbm.at[0], hid.at[zl_lo], hid_sem.at[zl_lo])
    own_hid.start()
    own_idx = pltpu.make_async_copy(idx_hbm, idx_rows, idx_sem)
    own_idx.start()
    rows = lax.broadcasted_iota(jnp.int32, (COLS, COLS), 0)
    cols = lax.broadcasted_iota(jnp.int32, (COLS, COLS), 1)
    signs = (1 - 2 * parity(rows & cols)).astype(jnp.float32).astype(jnp.bfloat16)
    for half in (0, 1):
        walsh[:, half * COLS : (half + 1) * COLS] = signs
        walsh_tall[half * COLS : (half + 1) * COLS, :] = signs
    acc[...] = jnp.zeros_like(acc)
    own_idx.wait()
    idx_wide[...] = jnp.zeros_like(idx_wide)
    for j in range(16):
        idx_wide[j : j + 1, :] = idx_rows[pl.ds(j * ROWS, ROWS)].reshape(1, ROWS) & 4095
    idx_cols[...] = idx_wide[...].T
    own_hid.wait()
    hid_t[zl_lo] = hid[zl_lo].T
    pl.semaphore_wait(barrier, 12 - jnp.where(s_self, 1, 0) - jnp.where(o_self, 1, 0))

    def slab(i):
        return pl.ds(i * SLAB, SLAB)

    def along_z(i, start):
        for t in (0, 1):
            args = (og_hbm.at[0, slab(i)], o_buf.at[zl_lo, y, c, slab(i)])
            send, recv = o_send.at[t, i], oz_sem.at[zl_lo, i]
            stays = jnp.logical_and(o_self, zh == t)

            @pl.when(jnp.logical_not(stays))
            def _():
                copy = remote(*args, send, recv, (x * 4 + o_to_zl, y * 4 + t * 2 + c))
                if start:
                    copy.start()
                else:
                    copy.wait_send()

            if start:

                @pl.when(stays)
                def _():
                    pltpu.make_async_copy(*args, recv).start()

        for t in (0, 1):
            s_args = (sc_hbm.at[slab(i)], s_buf.at[x, zl_lo, slab(i)])
            s_s, s_r = s_send.at[t, i], sz_sem.at[zl_lo, i]

            @pl.when(s_to[t] != zl)
            def _():
                copy = remote(*s_args, s_s, s_r, (x * 4 + s_to[t], par))
                if start:
                    copy.start()
                else:
                    copy.wait_send()

            if start:

                @pl.when(s_to[t] == zl)
                def _():
                    pltpu.make_async_copy(*s_args, s_r).start()

    hid_copy = remote(hid_hbm.at[0], hid.at[zl_lo], hid_send, hid_sem.at[zl_lo], hid_dev)

    def sx_copy(step, i):
        ref = s_buf.at[x, :, slab(i)]
        return remote(ref, ref, sx_send, sx_sem.at[step // 2, i], x_dev[step])

    def sf_copy(step, i):
        ref = s_buf.at[xs[4 - step], step // 2, slab(i)]
        return remote(ref, ref, sf_send, sf_sem.at[step // 2, i], x_dev[step])

    def oy_copy(step, i):
        ref = o_buf.at[:, y, c, slab(i)]
        return remote(ref, ref, oy_send, oy_sem.at[step // 2, i], y_dev[step])

    def of_copy(step, i):
        ref = o_buf.at[step // 2, ys[4 - step], c, slab(i)]
        return remote(ref, ref, of_send, of_sem.at[step // 2, i], y_dev[step])

    def sib_copy(step, i):
        ref = o_buf.at[:, ys[step], c, slab(i)]
        return remote(ref, ref, sib_send, sib_sem.at[step, i], sib_dev)

    def sib_wait(step, i):
        wait(o_buf.at[:, wrap(y + step, 4), 1 - c, slab(i)], sib_sem.at[step, i])

    def first(i):
        for d3 in (0, 1):
            wait(s_buf.at[x, d3, slab(i)], sz_sem.at[d3, i])
        for step in (1, 3):
            sx_copy(step, i).start()
        for e in (0, 1):
            wait(o_buf.at[e, y, c, slab(i)], oz_sem.at[e, i])
        for step in (1, 3):
            oy_copy(step, i).start()
        sib_copy(0, i).start()

    def second(i):
        for step in (1, 3):
            wait(s_buf.at[xs[4 - step], :, slab(i)], sx_sem.at[step // 2, i])
            sf_copy(step, i).start()
            wait(o_buf.at[:, ys[4 - step], c, slab(i)], oy_sem.at[step // 2, i])
            of_copy(step, i).start()
            sib_copy(4 - step, i).start()

    def third(i):
        for e in (0, 1):
            wait(o_buf.at[e, ys[2], c, slab(i)], of_sem.at[e, i])
        sib_copy(2, i).start()

    for i in range(min(WINDOW, CHUNKS)):
        along_z(i, True)
    for i in range(CHUNKS + 2):
        if i < CHUNKS:
            first(i)
        if i == HIDDEN_AT:
            for step in range(4):
                sib_wait(step, 0)
            hid_copy.start()
        if i < CHUNKS - WINDOW:
            along_z(i, False)
            along_z(i + WINDOW, True)
        if 0 < i <= CHUNKS:
            second(i - 1)
        if i > 1:
            third(i - 2)
    for i in range(CHUNKS):
        for d3 in (0, 1):
            wait(s_buf.at[xs[2], d3, slab(i)], sf_sem.at[d3, i])

    def tile(e, d1, d3):
        grad = jnp.dot(hid_t[e], o_buf[e, d1, d3], preferred_element_type=jnp.float32)
        weighted = grad * s_buf[d1, d3].astype(jnp.float32)
        top, low = weighted[: ROWS // 2], weighted[ROWS // 2 :]
        for half, part in ((0, top + low), (1, top - low)):
            hi = part.astype(jnp.bfloat16)
            lo = (part - hi.astype(jnp.float32)).astype(jnp.bfloat16)
            mixed = jnp.dot(walsh[...], jnp.concatenate([hi, lo], axis=0), preferred_element_type=jnp.float32)
            hi = mixed.astype(jnp.bfloat16)
            lo = (mixed - hi.astype(jnp.float32)).astype(jnp.bfloat16)
            mixed = jnp.dot(jnp.concatenate([hi, lo], axis=1), walsh_tall[...], preferred_element_type=jnp.float32)
            span = pl.ds(half * COLS, COLS)
            column = idx_cols[span, :]
            lane = column & 127
            left = jnp.take_along_axis(mixed[:, :128], lane, axis=1)
            right = jnp.take_along_axis(mixed[:, 128:], lane, axis=1)
            block = d1 * 4 + zl_lo * 2 + d3
            odd = parity((column >> 8) & block)
            value = jnp.where((column & 128) == 0, left, right)
            acc[e, span, :] += jnp.where(odd == 0, value, -value)

    def column_pair(e, step):
        d1 = wrap(y + step, 4)
        for d3 in (0, 1):
            tile(e, d1, d3)

    def own_columns(step, carry):
        for i in range(1, CHUNKS):
            sib_wait(step, i)
        column_pair(zl_lo, step)
        return carry

    lax.fori_loop(0, 4, own_columns, 0, unroll=True)

    own_slot = zl_lo * 16 + par
    other_slot = other_lo * 16

    def gather_picks(e):
        lines = acc[e].T
        j = lax.broadcasted_iota(jnp.int32, (16, 128), 0)
        sign = jnp.where(parity(j & par) == 0, SCALE, -SCALE)
        for q in range(4):
            red_out[e, :, q, :] = lines[:16, q * 128 : (q + 1) * 128] * sign

    def red_copy(e, step):
        there = wrap(par + step, 16)
        place = (jnp.where(e == zl_lo, ex, other_ex), there)
        return remote(red_out.at[e, there], red_in.at[own_slot], red_send, red_sem.at[own_slot], place)

    gather_picks(zl_lo)
    for step in range(1, 16):
        red_copy(zl_lo, step).start()
    red_in[own_slot] = red_out[zl_lo, par]

    wait(hid.at[other_lo], hid_sem.at[other_lo])
    hid_t[other_lo] = hid[other_lo].T

    def other_columns(step, carry):
        column_pair(other_lo, step)
        return carry

    lax.fori_loop(0, 4, other_columns, 0, unroll=True)
    gather_picks(other_lo)
    for step in range(16):
        red_copy(other_lo, step).start()

    for i in range(max(CHUNKS - WINDOW, 0), CHUNKS):
        along_z(i, False)
    hid_copy.wait_send()
    wait(s_buf.at[0:2], sx_send)
    wait(s_buf.at[0], sf_send)
    wait(s_buf.at[0:2], oy_send)
    wait(s_buf.at[0], of_send)
    wait(s_buf, sib_send)

    for step in range(16):
        there = wrap(par + step, 16)
        wait(red_in.at[other_slot + there], red_sem.at[other_slot + there])
        if step > 0:
            slot = zl_lo * 16 + there
            wait(red_in.at[slot], red_sem.at[slot])
    wait(red_in.at[0:31], red_send)
    total = jnp.sum(red_in[...], axis=0)
    for q in range(4):
        out_ref[:, q * 128 : (q + 1) * 128] = total[q : q + 1, :]


def local(hidden, out_grad, signed_scale, indices):
    dma = pltpu.SemaphoreType.DMA
    bf16, f32, i32 = jnp.bfloat16, jnp.float32, jnp.int32
    return pl.pallas_call(
        kernel,
        out_shape=jax.ShapeDtypeStruct((1, ROWS), f32),
        in_specs=[pl.BlockSpec(memory_space=pltpu.HBM)] * 4,
        out_specs=pl.BlockSpec(memory_space=pltpu.VMEM),
        scratch_shapes=[
            pltpu.VMEM((2, TOKENS, ROWS), bf16),
            pltpu.VMEM((2, ROWS, TOKENS), bf16),
            pltpu.VMEM((4, 2, ROWS, COLS), bf16),
            pltpu.VMEM((2, 4, 2, TOKENS, COLS), bf16),
            pltpu.VMEM((COLS, 2 * COLS), bf16),
            pltpu.VMEM((2 * COLS, COLS), bf16),
            pltpu.VMEM((8192,), i32),
            pltpu.VMEM((128, ROWS), i32),
            pltpu.VMEM((ROWS, 128), i32),
            pltpu.VMEM((2, ROWS, 128), f32),
            pltpu.VMEM((2, 16, 4, 128), f32),
            pltpu.VMEM((32, 4, 128), f32),
            dma((2,)),
            dma((2, CHUNKS)),
            dma((2, CHUNKS)),
            dma((2, CHUNKS)),
            dma((2, CHUNKS)),
            dma((2, CHUNKS)),
            dma((2, CHUNKS)),
            dma((4, CHUNKS)),
            dma(()),
            dma((32,)),
            dma(()),
            dma((2, CHUNKS)),
            dma((2, CHUNKS)),
            dma(()),
            dma(()),
            dma(()),
            dma(()),
            dma(()),
            dma(()),
        ],
        compiler_params=pltpu.CompilerParams(collective_id=0, has_side_effects=True, vmem_limit_bytes=56 << 20),
        cost_estimate=pl.CostEstimate(flops=6 << 30, bytes_accessed=8 << 20, transcendentals=0),
    )(hidden, out_grad, signed_scale, indices)


def solution(mesh):
    in_specs = (P("ex", None, "par"), P("ex", None, "par"), P("par", "ex"), P())
    out_specs = P("ex", "par")
    return jax.shard_map(local, mesh=mesh, in_specs=in_specs, out_specs=out_specs, check_vma=False)
```

```python
import jax
import jax.numpy as jnp
from jax import lax
from jax.experimental import pallas as pl
from jax.experimental.pallas import tpu as pltpu
from jax.sharding import PartitionSpec as P

MESH = pl.DeviceIdType.MESH
TOKENS = 512
ROWS = 512
COLS = 256
SCALE = 2.0**-17
CHUNKS = 4
WINDOW = 4
HIDDEN_AT = 2
SLAB = 512 // CHUNKS


def parity(bits):
    bits = bits ^ (bits >> 4)
    bits = bits ^ (bits >> 2)
    bits = bits ^ (bits >> 1)
    return bits & 1


def wrap(value, size):
    return jnp.where(value >= size, value - size, value)


def kernel(hid_hbm, og_hbm, sc_hbm, idx_hbm, out_ref, hid, hid_t, s_buf, o_buf, walsh, walsh_tall, idx_rows, idx_wide, idx_cols, acc,
           red_out, red_in, hid_sem, sz_sem, sx_sem, sf_sem, oz_sem, oy_sem, of_sem, sib_sem, idx_sem, red_sem, hid_send, s_send,
           o_send, sx_send, sf_send, oy_send, of_send, sib_send, red_send):
    ex = lax.axis_index("ex")
    par = lax.axis_index("par")
    x = ex // 4
    zl = ex - x * 4
    y = par // 4
    rest = par - y * 4
    zh = rest // 2
    c = rest - zh * 2
    zl_hi = zl // 2
    zl_lo = zl - zl_hi * 2
    other_lo = 1 - zl_lo
    other_ex = ex + 1 - 2 * zl_lo
    xs = [x, wrap(x + 1, 4), wrap(x + 2, 4), wrap(x + 3, 4)]
    ys = [y, wrap(y + 1, 4), wrap(y + 2, 4), wrap(y + 3, 4)]
    x_dev = [(ex + (v - x) * 4, par) for v in xs]
    y_dev = [(ex, par + (v - y) * 4) for v in ys]
    sib_dev = (ex, par + 1 - 2 * c)
    hid_dev = (other_ex, par)
    s_to = [2 * t + zl_hi for t in (0, 1)]
    s_from = [2 * zl_lo + d3 for d3 in (0, 1)]
    o_to_zl = zl_hi * 2 + zh
    o_from_zl = [zl_hi * 2 + e for e in (0, 1)]
    o_self = zh == zl_lo
    s_self = zl_hi == zl_lo

    def wait(ref, sem):
        pltpu.make_async_copy(ref, ref, sem).wait()

    def remote(src, dst, send, recv, place):
        return pltpu.make_async_remote_copy(src, dst, send, recv, device_id=place, device_id_type=MESH)

    barrier = pltpu.get_barrier_semaphore()

    def greet(place):
        pl.semaphore_signal(barrier, inc=1, device_id=place, device_id_type=MESH)

    for place in x_dev[1:] + y_dev[1:] + [sib_dev, hid_dev]:
        greet(place)
    for d3 in (0, 1):

        @pl.when(s_from[d3] != zl)
        def _():
            greet((x * 4 + s_from[d3], par))

    for e in (0, 1):

        @pl.when(jnp.logical_not(jnp.logical_and(o_self, zl_lo == e)))
        def _():
            greet((x * 4 + o_from_zl[e], y * 4 + zl_lo * 2 + c))

    own_hid = pltpu.make_async_copy(hid_hbm.at[0], hid.at[zl_lo], hid_sem.at[zl_lo])
    own_hid.start()
    own_idx = pltpu.make_async_copy(idx_hbm, idx_rows, idx_sem)
    own_idx.start()
    rows = lax.broadcasted_iota(jnp.int32, (COLS, COLS), 0)
    cols = lax.broadcasted_iota(jnp.int32, (COLS, COLS), 1)
    signs = (1 - 2 * parity(rows & cols)).astype(jnp.float32).astype(jnp.bfloat16)
    for half in (0, 1):
        walsh[:, half * COLS : (half + 1) * COLS] = signs
        walsh_tall[half * COLS : (half + 1) * COLS, :] = signs
    acc[...] = jnp.zeros_like(acc)
    own_idx.wait()
    idx_wide[...] = jnp.zeros_like(idx_wide)
    for j in range(16):
        idx_wide[j : j + 1, :] = idx_rows[pl.ds(j * ROWS, ROWS)].reshape(1, ROWS) & 4095
    idx_cols[...] = idx_wide[...].T
    own_hid.wait()
    hid_t[zl_lo] = hid[zl_lo].T
    pl.semaphore_wait(barrier, 12 - jnp.where(s_self, 1, 0) - jnp.where(o_self, 1, 0))

    def slab(i):
        return pl.ds(i * SLAB, SLAB)

    def along_z(i, start):
        for t in (0, 1):
            args = (og_hbm.at[0, slab(i)], o_buf.at[zl_lo, y, c, slab(i)])
            send, recv = o_send.at[t, i], oz_sem.at[zl_lo, i]
            stays = jnp.logical_and(o_self, zh == t)

            @pl.when(jnp.logical_not(stays))
            def _():
                copy = remote(*args, send, recv, (x * 4 + o_to_zl, y * 4 + t * 2 + c))
                if start:
                    copy.start()
                else:
                    copy.wait_send()

            if start:

                @pl.when(stays)
                def _():
                    pltpu.make_async_copy(*args, recv).start()

        for t in (0, 1):
            s_args = (sc_hbm.at[slab(i)], s_buf.at[x, zl_lo, slab(i)])
            s_s, s_r = s_send.at[t, i], sz_sem.at[zl_lo, i]

            @pl.when(s_to[t] != zl)
            def _():
                copy = remote(*s_args, s_s, s_r, (x * 4 + s_to[t], par))
                if start:
                    copy.start()
                else:
                    copy.wait_send()

            if start:

                @pl.when(s_to[t] == zl)
                def _():
                    pltpu.make_async_copy(*s_args, s_r).start()

    hid_copy = remote(hid_hbm.at[0], hid.at[zl_lo], hid_send, hid_sem.at[zl_lo], hid_dev)

    def sx_copy(step, i):
        ref = s_buf.at[x, :, slab(i)]
        return remote(ref, ref, sx_send, sx_sem.at[step // 2, i], x_dev[step])

    def sf_copy(step, i):
        ref = s_buf.at[xs[4 - step], step // 2, slab(i)]
        return remote(ref, ref, sf_send, sf_sem.at[step // 2, i], x_dev[step])

    def oy_copy(step, i):
        ref = o_buf.at[:, y, c, slab(i)]
        return remote(ref, ref, oy_send, oy_sem.at[step // 2, i], y_dev[step])

    def of_copy(step, i):
        ref = o_buf.at[step // 2, ys[4 - step], c, slab(i)]
        return remote(ref, ref, of_send, of_sem.at[step // 2, i], y_dev[step])

    def sib_copy(step, i):
        ref = o_buf.at[:, ys[step], c, slab(i)]
        return remote(ref, ref, sib_send, sib_sem.at[step, i], sib_dev)

    def sib_wait(step, i):
        wait(o_buf.at[:, wrap(y + step, 4), 1 - c, slab(i)], sib_sem.at[step, i])

    def first(i):
        for d3 in (0, 1):
            wait(s_buf.at[x, d3, slab(i)], sz_sem.at[d3, i])
        for step in (1, 3):
            sx_copy(step, i).start()
        for e in (0, 1):
            wait(o_buf.at[e, y, c, slab(i)], oz_sem.at[e, i])
        for step in (1, 3):
            oy_copy(step, i).start()
        sib_copy(0, i).start()

    def second(i):
        for step in (1, 3):
            wait(s_buf.at[xs[4 - step], :, slab(i)], sx_sem.at[step // 2, i])
            sf_copy(step, i).start()
            wait(o_buf.at[:, ys[4 - step], c, slab(i)], oy_sem.at[step // 2, i])
            of_copy(step, i).start()
            sib_copy(4 - step, i).start()

    def third(i):
        for e in (0, 1):
            wait(o_buf.at[e, ys[2], c, slab(i)], of_sem.at[e, i])
        sib_copy(2, i).start()

    for i in range(min(WINDOW, CHUNKS)):
        along_z(i, True)
    for i in range(CHUNKS + 2):
        if i < CHUNKS:
            first(i)
        if i < CHUNKS - WINDOW:
            along_z(i, False)
            along_z(i + WINDOW, True)
        if 0 < i <= CHUNKS:
            second(i - 1)
        if i > 1:
            third(i - 2)
        if i == HIDDEN_AT:
            for step in range(4):
                sib_wait(step, 0)
            hid_copy.start()
    for i in range(CHUNKS):
        for d3 in (0, 1):
            wait(s_buf.at[xs[2], d3, slab(i)], sf_sem.at[d3, i])

    def tile(e, d1, d3):
        grad = jnp.dot(hid_t[e], o_buf[e, d1, d3], preferred_element_type=jnp.float32)
        weighted = grad * s_buf[d1, d3].astype(jnp.float32)
        top, low = weighted[: ROWS // 2], weighted[ROWS // 2 :]
        for half, part in ((0, top + low), (1, top - low)):
            hi = part.astype(jnp.bfloat16)
            lo = (part - hi.astype(jnp.float32)).astype(jnp.bfloat16)
            mixed = jnp.dot(walsh[...], jnp.concatenate([hi, lo], axis=0), preferred_element_type=jnp.float32)
            hi = mixed.astype(jnp.bfloat16)
            lo = (mixed - hi.astype(jnp.float32)).astype(jnp.bfloat16)
            mixed = jnp.dot(jnp.concatenate([hi, lo], axis=1), walsh_tall[...], preferred_element_type=jnp.float32)
            span = pl.ds(half * COLS, COLS)
            column = idx_cols[span, :]
            lane = column & 127
            left = jnp.take_along_axis(mixed[:, :128], lane, axis=1)
            right = jnp.take_along_axis(mixed[:, 128:], lane, axis=1)
            block = d1 * 4 + zl_lo * 2 + d3
            odd = parity((column >> 8) & block)
            value = jnp.where((column & 128) == 0, left, right)
            acc[e, span, :] += jnp.where(odd == 0, value, -value)

    def column_pair(e, step):
        d1 = wrap(y + step, 4)
        for d3 in (0, 1):
            tile(e, d1, d3)

    def own_columns(step, carry):
        for i in range(1, CHUNKS):
            sib_wait(step, i)
        column_pair(zl_lo, step)
        return carry

    lax.fori_loop(0, 4, own_columns, 0, unroll=True)

    own_slot = zl_lo * 16 + par
    other_slot = other_lo * 16

    def gather_picks(e):
        lines = acc[e].T
        j = lax.broadcasted_iota(jnp.int32, (16, 128), 0)
        sign = jnp.where(parity(j & par) == 0, SCALE, -SCALE)
        for q in range(4):
            red_out[e, :, q, :] = lines[:16, q * 128 : (q + 1) * 128] * sign

    def red_copy(e, step):
        there = wrap(par + step, 16)
        place = (jnp.where(e == zl_lo, ex, other_ex), there)
        return remote(red_out.at[e, there], red_in.at[own_slot], red_send, red_sem.at[own_slot], place)

    gather_picks(zl_lo)
    for step in range(1, 16):
        red_copy(zl_lo, step).start()
    red_in[own_slot] = red_out[zl_lo, par]

    wait(hid.at[other_lo], hid_sem.at[other_lo])
    hid_t[other_lo] = hid[other_lo].T

    def other_columns(step, carry):
        column_pair(other_lo, step)
        return carry

    lax.fori_loop(0, 4, other_columns, 0, unroll=True)
    gather_picks(other_lo)
    for step in range(16):
        red_copy(other_lo, step).start()

    for i in range(max(CHUNKS - WINDOW, 0), CHUNKS):
        along_z(i, False)
    hid_copy.wait_send()
    wait(s_buf.at[0:2], sx_send)
    wait(s_buf.at[0], sf_send)
    wait(s_buf.at[0:2], oy_send)
    wait(s_buf.at[0], of_send)
    wait(s_buf, sib_send)

    for step in range(16):
        there = wrap(par + step, 16)
        wait(red_in.at[other_slot + there], red_sem.at[other_slot + there])
        if step > 0:
            slot = zl_lo * 16 + there
            wait(red_in.at[slot], red_sem.at[slot])
    wait(red_in.at[0:31], red_send)
    total = jnp.sum(red_in[...], axis=0)
    for q in range(4):
        out_ref[:, q * 128 : (q + 1) * 128] = total[q : q + 1, :]


def local(hidden, out_grad, signed_scale, indices):
    dma = pltpu.SemaphoreType.DMA
    bf16, f32, i32 = jnp.bfloat16, jnp.float32, jnp.int32
    return pl.pallas_call(
        kernel,
        out_shape=jax.ShapeDtypeStruct((1, ROWS), f32),
        in_specs=[pl.BlockSpec(memory_space=pltpu.HBM)] * 4,
        out_specs=pl.BlockSpec(memory_space=pltpu.VMEM),
        scratch_shapes=[
            pltpu.VMEM((2, TOKENS, ROWS), bf16),
            pltpu.VMEM((2, ROWS, TOKENS), bf16),
            pltpu.VMEM((4, 2, ROWS, COLS), bf16),
            pltpu.VMEM((2, 4, 2, TOKENS, COLS), bf16),
            pltpu.VMEM((COLS, 2 * COLS), bf16),
            pltpu.VMEM((2 * COLS, COLS), bf16),
            pltpu.VMEM((8192,), i32),
            pltpu.VMEM((128, ROWS), i32),
            pltpu.VMEM((ROWS, 128), i32),
            pltpu.VMEM((2, ROWS, 128), f32),
            pltpu.VMEM((2, 16, 4, 128), f32),
            pltpu.VMEM((32, 4, 128), f32),
            dma((2,)),
            dma((2, CHUNKS)),
            dma((2, CHUNKS)),
            dma((2, CHUNKS)),
            dma((2, CHUNKS)),
            dma((2, CHUNKS)),
            dma((2, CHUNKS)),
            dma((4, CHUNKS)),
            dma(()),
            dma((32,)),
            dma(()),
            dma((2, CHUNKS)),
            dma((2, CHUNKS)),
            dma(()),
            dma(()),
            dma(()),
            dma(()),
            dma(()),
            dma(()),
        ],
        compiler_params=pltpu.CompilerParams(collective_id=0, has_side_effects=True, vmem_limit_bytes=56 << 20),
        cost_estimate=pl.CostEstimate(flops=6 << 30, bytes_accessed=8 << 20, transcendentals=0),
    )(hidden, out_grad, signed_scale, indices)


def solution(mesh):
    in_specs = (P("ex", None, "par"), P("ex", None, "par"), P("par", "ex"), P())
    out_specs = P("ex", "par")
    return jax.shard_map(local, mesh=mesh, in_specs=in_specs, out_specs=out_specs, check_vma=False)
```
